256 devices in a mesh: dp: 16 (over x, z_lo), ctx: 16 (over z_hi, y, core).
Axes of the slice: x: 4, y: 4, z: 8 (z_hi: 2, z_lo: 4; z = z_hi * 4 + z_lo), core: 2. Of those that a mesh axis runs over, the one named last changes fastest.
Arguments:
- normed_layer_input: bfloat16 [32768, 4096], P(('dp', 'ctx')), may hold values from -6 to 6
- saved_query_state: bfloat16 [32768, 2048], P(('dp', 'ctx')), may hold values from -105 to 105
- saved_key_state: bfloat16 [32768, 512], P(('dp', 'ctx')), may hold values from -3.8 to 3.8
- saved_value_state: bfloat16 [32768, 512], P(('dp', 'ctx')), may hold values from -6 to 6
- output_cotangent: bfloat16 [32768, 2048], P(('dp', 'ctx')), may hold values from -0.5 to 0.5
- document_lengths: int32 [16, 8], P('dp'), may hold values from 1 to 1024, 2048 in all within a row
- span_order: int32 [32], replicated, may hold values from 0 to 31, each once
Outputs:
- grad_query_weight: float32 [4096, 2048], P('ctx')
- grad_key_weight: float32 [4096, 512], P('ctx')
- grad_value_weight: float32 [4096, 512], P('ctx')
The draws below stay inside these ranges and needn't reach their ends.
Inputs may be any that keep to these rules, and one draw needn't show every extreme that they name: `document_lengths`: each sequence's 8 lengths sum to 2048, and one of them is exactly 1024. `span_order`: a permutation: every position block of a sequence is stored once.
All inputs are finite; a program needn't handle non-finite values.
Results may differ from the reference program's by a relative error of at most 0.024.
Values may be sent and summed in bfloat16 or wider, within the bound.
No kernel may reach another device: no remote copies, remote signals or barrier semaphores. Data moves between devices by JAX's collectives and lax.ppermute only.
A program may use at most 64 MiB of HBM per device.

```python
import math
import jax
import jax.numpy as jnp
import numpy as np
from jax import lax

MODEL_WIDTH = 4096
QUERY_HEADS = 16
KEY_VALUE_HEADS = 4
HEAD_WIDTH = 128
TOKENS_PER_PART = 128
DOCS = 8
SEQUENCE_TOKENS = 2048
GROUPS = 16
TOKEN_TOTAL = 32768
HALF = 64
SPANS = 32
LONGEST = 1024
N_DP = 16
N_CTX = 16


def key_base(key):
    base_offset = jax.random.normal(jax.random.fold_in(key, 11), (TOKEN_TOTAL, KEY_VALUE_HEADS * HEAD_WIDTH), jnp.float32)
    return jnp.clip(base_offset, -3.5, 3.5)


def draw_saved_key_state(key, part):
    base_offset = key_base(key)
    return base_offset.astype(jnp.bfloat16)


def draw_saved_query_state(key, part):
    key = jax.random.fold_in(key, 5)
    query_block = jnp.clip(jax.random.normal(key, (TOKEN_TOTAL, QUERY_HEADS * HEAD_WIDTH), jnp.float32), -3.5, 3.5)
    return query_block.astype(jnp.bfloat16)


def level_of(key, extent, split, low, high):
    gain = 1.0
    for axis_at, parts in split:
        draws = jax.random.uniform(jax.random.fold_in(jax.random.fold_in(key, 6), axis_at), (parts,), jnp.float32, low / len(split), high / len(split))
        gain = gain * jnp.repeat(jnp.exp(draws), extent[axis_at] // parts).reshape((-1,) + (1,) * (len(extent) - 1 - axis_at))
    return gain


def length_profile(number_of, total, most, slope):
    loads = [(1 << 20) // math.isqrt(grade ** slope) + 1 for grade in range(2, number_of + 1)]
    spare, given = total - most - (number_of - 1), [1] * (number_of - 1)
    while spare > 0:
        candidates = [i for i in range(number_of - 1) if given[i] < most]
        whole, remaining = sum([loads[i] for i in candidates]), spare
        for i in candidates:
            extra = min(most - given[i], max(1, remaining * loads[i] // whole), spare)
            given[i] = given[i] + extra
            spare = spare - extra
    return np.array([most] + given)


def uneven_parts(own_key, count, total, bound, slope):
    if count == 2:
        one = jax.random.randint(own_key, (), max(1, total - bound), min(bound, total - 1) + 1)
        return jnp.stack([one, total - one])
    sizes = jnp.asarray(length_profile(count, total, bound, slope), jnp.int32)
    twos = (count - 1) // 2
    donor, receiver = sizes[1:1 + 2 * twos:2], sizes[2:2 + 2 * twos:2]
    room = jnp.minimum(donor - 1, bound - receiver)
    shifted = jax.random.randint(jax.random.fold_in(own_key, 1), (twos,), 0, 1 << 20) % (room + 1)
    sizes = sizes.at[1:1 + 2 * twos:2].set(donor - shifted).at[2:2 + 2 * twos:2].set(receiver + shifted)
    return sizes[jax.random.permutation(jax.random.fold_in(own_key, 2), count)]


def centred(key, extent, deviation, reach, pieces=(), kind=jnp.bfloat16):
    loudness = level_of(key, extent, pieces, -0.22, 0.18) if pieces else 1.0
    result = jax.random.normal(key, extent, jnp.float32) * deviation * loudness
    return jnp.minimum(jnp.maximum(result, -reach), reach).astype(kind)


def setup_inputs(seed: int = 0) -> dict:
    key_list = jax.random.split(jax.random.key(seed), 8)
    normed_layer_input = centred(key_list[0], (TOKEN_TOTAL, MODEL_WIDTH), 1.0, 6.0, ((0, 256),))
    saved_query_state = draw_saved_query_state(jax.random.fold_in(key_list[7], 71), 0)
    saved_key_state = draw_saved_key_state(jax.random.fold_in(key_list[7], 71), 0)
    saved_value_state = centred(key_list[3], (TOKEN_TOTAL, KEY_VALUE_HEADS * HEAD_WIDTH), 1.0, 6.0, ((0, 256),))
    output_cotangent = centred(key_list[4], (TOKEN_TOTAL, QUERY_HEADS * HEAD_WIDTH), (TOKEN_TOTAL // 256) ** -0.5, 0.5, ((0, 256),))
    document_lengths = jax.vmap(lambda own: uneven_parts(own, DOCS, SEQUENCE_TOKENS, LONGEST, 2))(jax.random.split(key_list[5], GROUPS)).reshape((GROUPS, DOCS)).astype(jnp.int32)
    span_order = jax.random.permutation(key_list[6], SPANS).astype(jnp.int32)
    return dict(normed_layer_input=normed_layer_input, saved_query_state=saved_query_state, saved_key_state=saved_key_state, saved_value_state=saved_value_state, output_cotangent=output_cotangent, document_lengths=document_lengths, span_order=span_order)


def rounded(values):
    return lax.optimization_barrier(values.astype(jnp.bfloat16)).astype(jnp.float32)

def storage_positions(span_order):
    row_index = jnp.arange(SEQUENCE_TOKENS, dtype=jnp.int32)
    return span_order[row_index // HALF] * HALF + row_index % HALF

def doc_numbers(positions, lengths):
    doc_ends = jnp.cumsum(lengths, dtype=jnp.int32)
    return lax.optimization_barrier(jnp.sum((positions[:, None] >= doc_ends[None, :]).astype(jnp.int32), axis=1, dtype=jnp.int32))

def block_grads(query_row_block, output_rows, key_row_block, value_row_block, visible):
    group_width = QUERY_HEADS // KEY_VALUE_HEADS
    score_scale = 1.0 / math.sqrt(HEAD_WIDTH)
    query_block = query_row_block.astype(jnp.float32).reshape(TOKENS_PER_PART, KEY_VALUE_HEADS, group_width, HEAD_WIDTH)
    output_gradient = output_rows.astype(jnp.float32).reshape(TOKENS_PER_PART, KEY_VALUE_HEADS, group_width, HEAD_WIDTH)
    key_head_rows = key_row_block.astype(jnp.float32).reshape(SEQUENCE_TOKENS, KEY_VALUE_HEADS, HEAD_WIDTH)
    value_head_rows = value_row_block.astype(jnp.float32).reshape(SEQUENCE_TOKENS, KEY_VALUE_HEADS, HEAD_WIDTH)
    scores = jnp.einsum('tkgd,skd->kgts', query_block, key_head_rows) * score_scale
    masked = jnp.where(visible[None, None], scores, -jnp.inf)
    row_max = lax.optimization_barrier(jnp.max(masked, axis=3, keepdims=True))
    weights = jnp.where(visible[None, None], jnp.exp(masked - row_max), 0.0)
    probability = weights / lax.optimization_barrier(jnp.sum(weights, axis=3, keepdims=True))
    prob_half = rounded(probability)
    prob_grad = jnp.einsum('tkgd,skd->kgts', output_gradient, value_head_rows)
    row_delta = lax.optimization_barrier(jnp.sum(probability * prob_grad, axis=3, keepdims=True))
    score_grad = rounded(probability * (prob_grad - row_delta))
    query_gradient = jnp.einsum('kgts,skd->tkgd', score_grad, key_head_rows) * score_scale
    key_portion = jnp.einsum('kgts,tkgd->skd', score_grad, query_block) * score_scale
    value_portion = jnp.einsum('kgts,tkgd->skd', prob_half, output_gradient)
    return (query_gradient.reshape(TOKENS_PER_PART, QUERY_HEADS * HEAD_WIDTH).astype(jnp.bfloat16), key_portion.reshape(SEQUENCE_TOKENS, KEY_VALUE_HEADS * HEAD_WIDTH).astype(jnp.bfloat16), value_portion.reshape(SEQUENCE_TOKENS, KEY_VALUE_HEADS * HEAD_WIDTH).astype(jnp.bfloat16))

def reference(normed_layer_input, saved_query_state, saved_key_state, saved_value_state, output_cotangent, document_lengths, span_order):
    positions = storage_positions(span_order)

    def group_grads(carry_sum, group_payload):
        inputs, query_block, key_row_block, value_row_block, output_gradient, lengths = group_payload
        documents = doc_numbers(positions, lengths)

        def one_block(block_index):
            first_row = block_index * TOKENS_PER_PART
            query_pos = lax.dynamic_slice_in_dim(positions, first_row, TOKENS_PER_PART)
            query_doc = lax.dynamic_slice_in_dim(documents, first_row, TOKENS_PER_PART)
            visible = (positions[None, :] <= query_pos[:, None]) & (documents[None, :] == query_doc[:, None])
            query_row_block = lax.dynamic_slice_in_dim(query_block, first_row, TOKENS_PER_PART)
            output_rows = lax.dynamic_slice_in_dim(output_gradient, first_row, TOKENS_PER_PART)
            return block_grads(query_row_block, output_rows, key_row_block, value_row_block, visible)
        query_gradient, key_parts, value_parts = lax.map(one_block, jnp.arange(N_CTX, dtype=jnp.int32))
        query_gradient = query_gradient.reshape(SEQUENCE_TOKENS, QUERY_HEADS * HEAD_WIDTH)
        key_grad = lax.optimization_barrier(jnp.sum(key_parts.astype(jnp.float32), axis=0)).astype(jnp.bfloat16)
        value_grad = lax.optimization_barrier(jnp.sum(value_parts.astype(jnp.float32), axis=0)).astype(jnp.bfloat16)
        grads = jnp.concatenate([query_gradient, key_grad, value_grad], axis=1)
        return (carry_sum + jnp.dot(inputs.T, grads, preferred_element_type=jnp.float32), None)
    group_payload = (normed_layer_input.reshape(N_DP, SEQUENCE_TOKENS, MODEL_WIDTH), saved_query_state.reshape(N_DP, SEQUENCE_TOKENS, QUERY_HEADS * HEAD_WIDTH), saved_key_state.reshape(N_DP, SEQUENCE_TOKENS, KEY_VALUE_HEADS * HEAD_WIDTH), saved_value_state.reshape(N_DP, SEQUENCE_TOKENS, KEY_VALUE_HEADS * HEAD_WIDTH), output_cotangent.reshape(N_DP, SEQUENCE_TOKENS, QUERY_HEADS * HEAD_WIDTH), document_lengths)
    starting_offsets = jnp.zeros((MODEL_WIDTH, (QUERY_HEADS + 2 * KEY_VALUE_HEADS) * HEAD_WIDTH), jnp.float32)
    overall_total, unused = lax.scan(group_grads, starting_offsets, group_payload)
    return (overall_total[:, :QUERY_HEADS * HEAD_WIDTH], overall_total[:, QUERY_HEADS * HEAD_WIDTH:(QUERY_HEADS + KEY_VALUE_HEADS) * HEAD_WIDTH], overall_total[:, (QUERY_HEADS + KEY_VALUE_HEADS) * HEAD_WIDTH:])
```

```python
import functools
import math

import jax
import jax.numpy as jnp
from jax import lax
from jax.experimental import pallas as pl
from jax.experimental.pallas import tpu as pltpu
from jax.sharding import Mesh, PartitionSpec as P

HEAD = 128
KV_HEADS = 4
HALF = 64
SPANS = 32
SEQ = 2048
NX, NZL, NZH, NY, NC = 4, 4, 2, 4, 2
ROWS = 128
OWN = ROWS * NY * NC
FEATS = 256
SCALE = 1.0 / math.sqrt(HEAD)
LOG2E = math.log2(math.e)
TILE = 256
VMEM = 56 * 1024 * 1024
AXES = ("x", "zl", "zh", "y", "c")


def nt(a, b):
    return lax.dot_general(a, b, (((1,), (1,)), ((), ())), preferred_element_type=jnp.float32)


def tn(a, b):
    return lax.dot_general(a, b, (((0,), (0,)), ((), ())), preferred_element_type=jnp.float32)


def nn(a, b):
    return lax.dot_general(a, b, (((1,), (0,)), ((), ())), preferred_element_type=jnp.float32)


def attention_kernel(ids, span, lens, own, other, dq_ref, dkv_ref, ks, vs, dk, dv):
    zh, core = ids[0], ids[1]
    blocks = OWN // HALF
    for j in range(blocks):
        rows = slice((j % 2) * HALF, (j % 2) * HALF + HALF)
        at = pl.ds(pl.multiple_of(span[zh * blocks + j] * HALF, HALF), HALF)
        ks[at, :] = own[j // 2, rows, 4 * HEAD : 5 * HEAD]
        vs[at, :] = own[j // 2, rows, 5 * HEAD : 6 * HEAD]
        at = pl.ds(pl.multiple_of(span[(1 - zh) * blocks + j] * HALF, HALF), HALF)
        ks[at, :] = other[j // 2, rows, :HEAD]
        vs[at, :] = other[j // 2, rows, HEAD:]
    dk[...] = jnp.zeros_like(dk)
    dv[...] = jnp.zeros_like(dv)
    ends = []
    total = jnp.int32(0)
    for d in range(lens.shape[1]):
        total = total + lens[0, d]
        ends.append(total)
    lane = lax.broadcasted_iota(jnp.int32, (1, 2 * HALF), 1) % HALF

    def block(j, carry):
        first = span[zh * blocks + j] * HALF
        low = jnp.int32(0)
        for e in ends:
            low = jnp.where(e <= first, e, low)
        high = pl.cdiv(first + HALF, 2 * HALF) * (2 * HALF)
        tiles = pl.cdiv(high - low, TILE)
        half, part = j // 2, pl.multiple_of((j % 2) * HALF, HALF)
        q = jnp.concatenate(
            [own[half, pl.ds(part, HALF), :HEAD], own[half, pl.ds(part, HALF), HEAD : 2 * HEAD]], axis=0
        )
        do = jnp.concatenate(
            [own[half, pl.ds(part, HALF), 2 * HEAD : 3 * HEAD], own[half, pl.ds(part, HALF), 3 * HEAD : 4 * HEAD]],
            axis=0,
        )
        pos = first + lane
        doc = jnp.zeros_like(pos)
        for e in ends:
            doc = jnp.where(e <= pos, e, doc)

        def work(n):
            keys = n * TILE
            start = pl.multiple_of(jnp.maximum(high - keys, 0), 2 * HALF)
            at = pl.ds(start, keys)
            k, v = ks[at, :], vs[at, :]
            row = lax.broadcasted_iota(jnp.int32, (keys, 2 * HALF), 0)
            seen = (row >= doc - start) & (row <= pos - start)
            s = jnp.where(seen, nt(k, q), -1e30)
            top = jnp.max(s, axis=0, keepdims=True)
            p = jnp.exp2((s - top) * (SCALE * LOG2E))
            p = p * (1.0 / jnp.sum(p, axis=0, keepdims=True))
            dp = nt(v, do)
            delta = jnp.sum(p * dp, axis=0, keepdims=True)
            ds = (p * (dp - delta)).astype(jnp.bfloat16)
            dv[at, :] += nn(p.astype(jnp.bfloat16), do)
            dk[at, :] += nn(ds, q)
            g = (tn(ds, k) * SCALE).astype(jnp.bfloat16)
            out = pl.ds(pl.multiple_of(j * HALF, HALF), HALF)
            dq_ref[out, :HEAD] = g[:HALF]
            dq_ref[out, HEAD:] = g[HALF:]

        for n in range(1, 6):
            pl.when(tiles == n)(functools.partial(work, n))
        return carry

    lax.fori_loop(0, blocks, block, 0)
    for j in range(blocks):
        for side, base in ((zh, 0), (1 - zh, OWN)):
            at = pl.ds(pl.multiple_of(span[side * blocks + j] * HALF, HALF), HALF)
            to = slice(base + j * HALF, base + (j + 1) * HALF)
            dkv_ref[core, to, :] = (dk[at, :] * SCALE).astype(jnp.bfloat16)
            dkv_ref[1 - core, to, :] = dv[at, :].astype(jnp.bfloat16)


def attention(ids, span, lens, own, other):
    smem = pl.BlockSpec(memory_space=pltpu.SMEM)
    vmem = pl.BlockSpec(memory_space=pltpu.VMEM)
    return pl.pallas_call(
        attention_kernel,
        out_shape=(
            jax.ShapeDtypeStruct((OWN, 2 * HEAD), jnp.bfloat16),
            jax.ShapeDtypeStruct((2, SEQ, HEAD), jnp.bfloat16),
        ),
        in_specs=[smem, smem, smem, vmem, vmem],
        out_specs=(vmem, vmem),
        scratch_shapes=[
            pltpu.VMEM((SEQ, HEAD), jnp.bfloat16),
            pltpu.VMEM((SEQ, HEAD), jnp.bfloat16),
            pltpu.VMEM((SEQ, HEAD), jnp.float32),
            pltpu.VMEM((SEQ, HEAD), jnp.float32),
        ],
        compiler_params=pltpu.CompilerParams(vmem_limit_bytes=VMEM),
        name="attention_backward",
    )(ids, span, lens, own, other)


def weight_kernel(x_ref, g_ref, out_ref):
    r = tn(x_ref[...], g_ref[...]).astype(jnp.bfloat16)
    out_ref[:, 0, 0] = r.reshape(out_ref.shape[0], out_ref.shape[3], out_ref.shape[4])


def weight_term(x, g):
    cols = g.shape[1]
    return pl.pallas_call(
        weight_kernel,
        grid=(NZH * NY,),
        out_shape=jax.ShapeDtypeStruct((NX, NY, NZH, FEATS // NX, cols), jnp.bfloat16),
        in_specs=[
            pl.BlockSpec((OWN, FEATS), lambda i: (0, i)),
            pl.BlockSpec((OWN, cols), lambda i: (0, 0)),
        ],
        out_specs=pl.BlockSpec((NX, 1, 1, FEATS // NX, cols), lambda i: (0, i % NY, i // NY, 0, 0)),
        compiler_params=pltpu.CompilerParams(vmem_limit_bytes=VMEM),
        name="weight_term",
    )(x, g)


def finish_kernel(ids, a, b, c, d, q_ref, k_ref, v_ref):
    x, zl = ids[0], ids[1]
    sub = FEATS // (NX * NZL)
    cols = KV_HEADS * HEAD
    for sx, piece in enumerate((a, b, c, d)):
        for sz in range(NZL):
            row = lax.rem(x - sx + NX, NX) * (FEATS // NX) + lax.rem(zl - sz + NZL, NZL) * sub
            at = pl.ds(pl.multiple_of(row, sub), sub)
            for y in range(NY):
                got = piece[sz, y].astype(jnp.float32)
                q_ref[at, y * cols : (y + 1) * cols] = got[:, :cols]
                k_ref[at, y * HEAD : (y + 1) * HEAD] = got[:, cols : cols + HEAD]
                v_ref[at, y * HEAD : (y + 1) * HEAD] = got[:, cols + HEAD :]


def finish(ids, pieces):
    smem = pl.BlockSpec(memory_space=pltpu.SMEM)
    vmem = pl.BlockSpec(memory_space=pltpu.VMEM)
    cols = KV_HEADS * HEAD
    return pl.pallas_call(
        finish_kernel,
        out_shape=(
            jax.ShapeDtypeStruct((FEATS, NY * cols), jnp.float32),
            jax.ShapeDtypeStruct((FEATS, cols), jnp.float32),
            jax.ShapeDtypeStruct((FEATS, cols), jnp.float32),
        ),
        in_specs=[smem, vmem, vmem, vmem, vmem],
        out_specs=(vmem, vmem, vmem),
        compiler_params=pltpu.CompilerParams(vmem_limit_bytes=VMEM),
        name="finish",
    )(ids, *pieces)


def shift(value, axis, n, s):
    return lax.ppermute(value, axis, [(i, (i + s) % n) for i in range(n)])


def by_head(value, copies):
    return jnp.broadcast_to(value.reshape(ROWS, KV_HEADS, 1, HEAD), (ROWS, KV_HEADS, copies, HEAD)).reshape(
        ROWS, KV_HEADS * copies, HEAD
    )


def in_order(first, mine, got, axis):
    return jnp.where(
        first, jnp.concatenate([mine, got], axis=axis), jnp.concatenate([got, mine], axis=axis)
    )


def reduce_term(term):
    cols = term.shape[-1]
    sub = FEATS // (NX * NZL)
    got = lax.all_to_all(term.reshape(NX * NY, NZH * FEATS // NX, cols), ("x", "y"), 0, 0, tiled=True)
    got = got.reshape(NX, NY, NZH, NZL, sub, cols)
    part = jnp.sum(got.astype(jnp.float32), axis=0).astype(jnp.bfloat16)
    part = part.transpose(1, 2, 0, 3, 4).reshape(NZH * NZL, NY * sub, cols)
    got = lax.all_to_all(part, ("zh", "zl"), 0, 0, tiled=True).reshape(NZH * NZL, NY, sub, cols)
    return jnp.sum(got.astype(jnp.float32), axis=0).astype(jnp.bfloat16)


def shards(x, q, k, v, do, lens, span):
    ix, izl, izh, core = (lax.axis_index(a) for a in ("x", "zl", "zh", "c"))
    first = core == 0
    groups = NY * NC

    kv_other = shift(jnp.concatenate([k, v], axis=1), "zh", NZH, 1)
    send = jnp.concatenate(
        [
            q.reshape(ROWS, groups, 2 * HEAD),
            do.reshape(ROWS, groups, 2 * HEAD),
            by_head(k, NC),
            by_head(v, NC),
        ],
        axis=2,
    ).transpose(1, 0, 2)
    own = lax.all_to_all(send, ("y", "c"), 0, 0, tiled=True)
    k_o, v_o = kv_other[:, : KV_HEADS * HEAD], kv_other[:, KV_HEADS * HEAD :]
    send = jnp.concatenate([by_head(k_o, NC), by_head(v_o, NC)], axis=2).transpose(1, 0, 2)
    other = lax.all_to_all(send, ("y", "c"), 0, 0, tiled=True)

    by_class = x.reshape(ROWS, NZH * NY, NC, FEATS)
    keep = jnp.where(first, by_class[:, :, 0], by_class[:, :, 1]).reshape(ROWS, -1)
    give = jnp.where(first, by_class[:, :, 1], by_class[:, :, 0]).reshape(ROWS, -1)
    pair = in_order(first, keep, shift(give, "c", NC, 1), 0)
    x_all = lax.all_gather(pair, "y", axis=0, tiled=True)

    dq, dkv = attention(jnp.stack([izh, core]).astype(jnp.int32), span, lens, own, other)

    gq = in_order(first, dq, shift(dq, "c", NC, 1), 1)
    got = shift(dkv[1], "c", NC, 1)
    both = dkv[0].astype(jnp.float32) + got.astype(jnp.float32)
    got = shift(both[OWN:].astype(jnp.bfloat16), "zh", NZH, 1)
    mine = (both[:OWN] + got.astype(jnp.float32)).astype(jnp.bfloat16)
    gkv = in_order(first, mine, shift(mine, "c", NC, 1), 1)

    piece = jnp.concatenate(
        [reduce_term(weight_term(x_all, gq)), reduce_term(weight_term(x_all, gkv))], axis=2
    )
    line = jnp.stack([piece] + [shift(piece, "zl", NZL, s) for s in range(1, NZL)])
    pieces = [line] + [shift(line, "x", NX, s) for s in range(1, NX)]
    return finish(jnp.stack([ix, izl]).astype(jnp.int32), pieces)


def solution(mesh):
    fine = Mesh(mesh.devices.reshape(NX, NZL, NZH, NY, NC), AXES)
    rows = P(AXES, None)
    out = P(("zh", "y", "c"), None)
    return jax.shard_map(
        shards,
        mesh=fine,
        in_specs=(rows, rows, rows, rows, rows, P(("x", "zl"), None), P()),
        out_specs=(out, out, out),
        check_vma=False,
    )
```

```python
import functools
import math

import jax
import jax.numpy as jnp
from jax import lax
from jax.experimental import pallas as pl
from jax.experimental.pallas import tpu as pltpu
from jax.sharding import Mesh, PartitionSpec as P

HEAD = 128
KV_HEADS = 4
HALF = 64
SPANS = 32
SEQ = 2048
NX, NZL, NZH, NY, NC = 4, 4, 2, 4, 2
ROWS = 128
OWN = ROWS * NY * NC
FEATS = 256
SCALE = 1.0 / math.sqrt(HEAD)
LOG2E = math.log2(math.e)
TILE = 256
VMEM = 60 * 1024 * 1024
AXES = ("x", "zl", "zh", "y", "c")


def nt(a, b):
    return lax.dot_general(a, b, (((1,), (1,)), ((), ())), preferred_element_type=jnp.float32)


def tn(a, b):
    return lax.dot_general(a, b, (((0,), (0,)), ((), ())), preferred_element_type=jnp.float32)


def nn(a, b):
    return lax.dot_general(a, b, (((1,), (0,)), ((), ())), preferred_element_type=jnp.float32)


def cost(us):
    return pl.CostEstimate(flops=us * 1_000_000_000, bytes_accessed=us * 2_000_000, transcendentals=0)


def attention_kernel(ids, span, lens, own, kv, kv_got, dq_ref, keep_ref, give_ref, ks, vs, dk, dv):
    zh, core = ids[0], ids[1]
    blocks = OWN // HALF
    side = zh + core - 2 * zh * core
    for part, first in ((kv, side * blocks), (kv_got, (1 - side) * blocks)):
        for j in range(blocks):
            rows = slice((j % 2) * HALF, (j % 2) * HALF + HALF)
            at = pl.ds(pl.multiple_of(span[first + j] * HALF, HALF), HALF)
            ks[at, :] = part[j // 2, rows, :HEAD]
            vs[at, :] = part[j // 2, rows, HEAD:]
    dk[...] = jnp.zeros_like(dk)
    dv[...] = jnp.zeros_like(dv)
    ends = []
    total = jnp.int32(0)
    for d in range(lens.shape[1]):
        total = total + lens[0, d]
        ends.append(total)
    lane = lax.broadcasted_iota(jnp.int32, (1, 2 * HALF), 1) % HALF

    def block(j, carry):
        first = span[zh * blocks + j] * HALF
        low = jnp.int32(0)
        for e in ends:
            low = jnp.where(e <= first, e, low)
        high = pl.cdiv(first + HALF, 2 * HALF) * (2 * HALF)
        tiles = pl.cdiv(high - low, TILE)
        half, part = j // 2, pl.multiple_of((j % 2) * HALF, HALF)
        q = jnp.concatenate(
            [own[half, pl.ds(part, HALF), :HEAD], own[half, pl.ds(part, HALF), HEAD : 2 * HEAD]], axis=0
        )
        do = jnp.concatenate(
            [own[half, pl.ds(part, HALF), 2 * HEAD : 3 * HEAD], own[half, pl.ds(part, HALF), 3 * HEAD : 4 * HEAD]],
            axis=0,
        )
        pos = first + lane
        doc = jnp.zeros_like(pos)
        for e in ends:
            doc = jnp.where(e <= pos, e, doc)

        def work(n):
            keys = n * TILE
            start = pl.multiple_of(jnp.maximum(high - keys, 0), 2 * HALF)
            at = pl.ds(start, keys)
            k, v = ks[at, :], vs[at, :]
            row = lax.broadcasted_iota(jnp.int32, (keys, 2 * HALF), 0)
            seen = (row >= doc - start) & (row <= pos - start)
            s = jnp.where(seen, nt(k, q), -1e30)
            top = jnp.max(s, axis=0, keepdims=True)
            p = jnp.exp2((s - top) * (SCALE * LOG2E))
            p = p * (1.0 / jnp.sum(p, axis=0, keepdims=True))
            dp = nt(v, do)
            delta = jnp.sum(p * dp, axis=0, keepdims=True)
            ds = (p * (dp - delta)).astype(jnp.bfloat16)
            dv[at, :] += nn(p.astype(jnp.bfloat16), do)
            dk[at, :] += nn(ds, q)
            g = (tn(ds, k) * SCALE).astype(jnp.bfloat16)
            out = pl.ds(pl.multiple_of(j * HALF, HALF), HALF)
            dq_ref[out, :HEAD] = g[:HALF]
            dq_ref[out, HEAD:] = g[HALF:]

        for n in range(1, 6):
            pl.when(tiles == n)(functools.partial(work, n))
        return carry

    lax.fori_loop(0, blocks, block, 0)
    for which, a_ref, b_ref in ((0, keep_ref, give_ref), (1, give_ref, keep_ref)):

        @pl.when(core == which)
        def _(a_ref=a_ref, b_ref=b_ref):
            for j in range(blocks):
                for side, base in ((zh, 0), (1 - zh, OWN)):
                    at = pl.ds(pl.multiple_of(span[side * blocks + j] * HALF, HALF), HALF)
                    to = slice(base + j * HALF, base + (j + 1) * HALF)
                    a_ref[to, :] = (dk[at, :] * SCALE).astype(jnp.bfloat16)
                    b_ref[to, :] = dv[at, :].astype(jnp.bfloat16)


def attention(ids, span, lens, own, kv, kv_got):
    smem = pl.BlockSpec(memory_space=pltpu.SMEM)
    vmem = pl.BlockSpec(memory_space=pltpu.VMEM)
    return pl.pallas_call(
        attention_kernel,
        out_shape=(
            jax.ShapeDtypeStruct((OWN, 2 * HEAD), jnp.bfloat16),
            jax.ShapeDtypeStruct((SEQ, HEAD), jnp.bfloat16),
            jax.ShapeDtypeStruct((SEQ, HEAD), jnp.bfloat16),
        ),
        in_specs=[smem, smem, smem, vmem, vmem, vmem],
        out_specs=(vmem, vmem, vmem),
        cost_estimate=cost(14),
        scratch_shapes=[
            pltpu.VMEM((SEQ, HEAD), jnp.bfloat16),
            pltpu.VMEM((SEQ, HEAD), jnp.bfloat16),
            pltpu.VMEM((SEQ, HEAD), jnp.float32),
            pltpu.VMEM((SEQ, HEAD), jnp.float32),
        ],
        compiler_params=pltpu.CompilerParams(vmem_limit_bytes=VMEM),
        name="attention_backward",
    )(ids, span, lens, own, kv, kv_got)


def turn_kernel(ids, x_ref, keep, give, turned):
    core, x = ids[1], ids[2]
    rows = FEATS // NX
    for out, which in ((keep, core), (give, 1 - core)):
        for i in range(NZH * NY):
            turned[i % 2] = x_ref[:, pl.ds(pl.multiple_of((2 * i + which) * FEATS, FEATS), FEATS)].T
            for s in range(NX):
                at = pl.ds(pl.multiple_of(lax.rem(x + s, NX) * rows, rows), rows)
                out[s, i * rows : (i + 1) * rows, :] = turned[i % 2, at, :]


def turn(ids, x):
    smem = pl.BlockSpec(memory_space=pltpu.SMEM)
    vmem = pl.BlockSpec(memory_space=pltpu.VMEM)
    shape = jax.ShapeDtypeStruct((NX, NZH * NY * FEATS // NX, ROWS), jnp.bfloat16)
    return pl.pallas_call(
        turn_kernel,
        out_shape=(shape, shape),
        in_specs=[smem, vmem],
        out_specs=(vmem, vmem),
        scratch_shapes=[pltpu.VMEM((2, FEATS, ROWS), jnp.bfloat16)],
        compiler_params=pltpu.CompilerParams(vmem_limit_bytes=VMEM),
        name="turn",
    )(ids, x)


def weight_kernel(joined, ids, *refs):
    pieces, mine, got, out, g = refs[:8], refs[8 : 8 + NX], refs[8 + NX : 8 + 2 * NX], refs[-2], refs[-1]
    core, y = ids[1], ids[3]
    width = mine[0].shape[1]
    for i, s in enumerate((0, -1, 1, 2)):
        base = lax.rem(y + s + NY, NY) * (NC * ROWS)
        for t in range(NX):
            for half, which in enumerate((core, 1 - core)):
                at = pl.ds(pl.multiple_of(base + which * ROWS, ROWS), ROWS)
                to = slice((2 * t + half) * ROWS, (2 * t + half + 1) * ROWS)
                g[i, to, :width] = mine[t][at, :]
                g[i, to, width:] = got[t][at, :]
    sub = FEATS // (NX * NZL)
    first = 0
    if joined:
        before = refs[8 + 2 * NX]
        first = before.shape[-1]
        out[:, :, :, :, :first] = before[...]
    for zh in range(NZH):
        total = jnp.zeros((FEATS, 2 * width), jnp.float32)
        for i in range(NY):
            total += nn(pieces[4 * zh + i][...], g[i])
        total = total.astype(jnp.bfloat16)
        for y_to in range(NY):
            for zl in range(NZL):
                row = (y_to * NZL + zl) * sub
                out[zh, zl, y_to, :, first : first + 2 * width] = total[row : row + sub]


def weight_term(ids, xs, mine, got, before=None):
    width = mine[0].shape[1]
    cols = 2 * width + (before.shape[-1] if before is not None else 0)
    vmem = pl.BlockSpec(memory_space=pltpu.VMEM)
    more = [] if before is None else [before]
    return pl.pallas_call(
        functools.partial(weight_kernel, before is not None),
        out_shape=jax.ShapeDtypeStruct((NZH, NZL, NY, FEATS // (NX * NZL), cols), jnp.bfloat16),
        in_specs=[pl.BlockSpec(memory_space=pltpu.SMEM)] + [vmem] * (len(xs) + 2 * NX + len(more)),
        out_specs=vmem,
        scratch_shapes=[pltpu.VMEM((NY, OWN, 2 * width), jnp.bfloat16)],
        compiler_params=pltpu.CompilerParams(vmem_limit_bytes=VMEM),
        cost_estimate=cost(5),
        name="weight_term",
    )(ids, *xs, *mine, *got, *more)


def finish_kernel(ids, *refs):
    pieces, (q_ref, k_ref, v_ref) = refs[:NX], refs[NX:]
    core, x, zl = ids[1], ids[2], ids[4]
    sub = FEATS // (NX * NZL)
    for sx in range(NX):
        for sz in range(NZL):
            row = lax.rem(x - sx + NX, NX) * (FEATS // NX) + lax.rem(zl - sz + NZL, NZL) * sub
            at = pl.ds(pl.multiple_of(row, sub), sub)
            for y in range(NY):
                got = pieces[sx].at[sz, y]
                for i, which in enumerate((core, 1 - core)):
                    src = pl.ds(pl.multiple_of(which * 2 * HEAD, 2 * HEAD), 2 * HEAD)
                    to = slice((2 * y + i) * 2 * HEAD, (2 * y + i + 1) * 2 * HEAD)
                    q_ref[at, to] = got[:, src].astype(jnp.float32)
                    src = pl.ds(pl.multiple_of((4 + which) * HEAD, HEAD), HEAD)
                    (k_ref, v_ref)[i][at, y * HEAD : (y + 1) * HEAD] = got[:, src].astype(jnp.float32)


def finish(ids, pieces):
    smem = pl.BlockSpec(memory_space=pltpu.SMEM)
    vmem = pl.BlockSpec(memory_space=pltpu.VMEM)
    cols = KV_HEADS * HEAD
    return pl.pallas_call(
        finish_kernel,
        out_shape=(
            jax.ShapeDtypeStruct((FEATS, NY * cols), jnp.float32),
            jax.ShapeDtypeStruct((FEATS, cols), jnp.float32),
            jax.ShapeDtypeStruct((FEATS, cols), jnp.float32),
        ),
        in_specs=[smem] + [vmem] * len(pieces),
        out_specs=(vmem, vmem, vmem),
        compiler_params=pltpu.CompilerParams(vmem_limit_bytes=VMEM),
        name="finish",
    )(ids, *pieces)


def shift(value, axis, n, s):
    return lax.ppermute(value, axis, [(i, (i + s) % n) for i in range(n)])


def by_head(value, copies):
    return jnp.broadcast_to(value.reshape(ROWS, KV_HEADS, 1, HEAD), (ROWS, KV_HEADS, copies, HEAD)).reshape(
        ROWS, KV_HEADS * copies, HEAD
    )


def gather_x(value):
    return [value] + [shift(value, "x", NX, s) for s in range(1, NX)]


def other_core(values):
    rest = shift(jnp.concatenate(values[1:], axis=0), "c", NC, 1)
    n = values[0].shape[0]
    return [shift(values[0], "c", NC, 1)] + [rest[i * n : (i + 1) * n] for i in range(len(values) - 1)]


def shards(x, q, k, v, do, lens, span):
    ids = jnp.stack([lax.axis_index(a) for a in ("zh", "c", "x", "y", "zl")]).astype(jnp.int32)
    groups = NY * NC
    kv_rows = jnp.concatenate([k, v], axis=1)
    send = jnp.concatenate(
        [q.reshape(ROWS, groups, 2 * HEAD), do.reshape(ROWS, groups, 2 * HEAD)], axis=2
    ).transpose(1, 0, 2)
    kv_rows, x, send = lax.optimization_barrier((kv_rows, x, send))
    own = lax.all_to_all(send, ("y", "c"), 0, 0, tiled=True)
    far = shift(kv_rows, "zh", NZH, 1)

    keep, give = turn(ids, x)
    pair = jnp.concatenate([keep, shift(give, "c", NC, 1)], axis=2)
    quarters = [pair[0]] + [shift(pair[t], "x", NX, t) for t in range(1, NX)]
    xa, xb = (
        jnp.concatenate([t[h * FEATS : (h + 1) * FEATS] for t in quarters], axis=1) for h in range(NZH)
    )

    send = jnp.stack([kv_rows, far]).reshape(NC, ROWS, 2, KV_HEADS, HEAD)
    send = send.transpose(3, 0, 1, 2, 4).reshape(groups, ROWS, 2 * HEAD)
    own, send = lax.optimization_barrier((own, send))
    kv = lax.all_to_all(send, ("y", "c"), 0, 0, tiled=True)
    kv_got = shift(kv, "c", NC, 1)

    xa_up, xb_up = shift(xa, "y", NY, 1), shift(xb, "y", NY, 1)
    xa_down, xb_down = shift(xa, "y", NY, -1), shift(xb, "y", NY, -1)
    dq, kept, given = attention(ids, span, lens, own, kv, kv_got)
    dqs = gather_x(dq)
    both = kept.astype(jnp.float32) + shift(given, "c", NC, 1).astype(jnp.float32)
    got = shift(both[OWN:].astype(jnp.bfloat16), "zh", NZH, 1)
    got, xa_up, xb_down, xa_down, xb_up, *dqs = lax.optimization_barrier(
        (got, xa_up, xb_down, xa_down, xb_up, *dqs)
    )
    xa_far, xb_far = shift(xa_up, "y", NY, 1), shift(xb_down, "y", NY, -1)
    x_all = [xa, xa_up, xa_down, xa_far, xb, xb_up, xb_down, xb_far]
    mine = (both[:OWN] + got.astype(jnp.float32)).astype(jnp.bfloat16)
    mines = gather_x(mine)
    part = weight_term(ids, x_all, dqs, other_core(dqs))
    part, *mines = lax.optimization_barrier((part, *mines))
    part = weight_term(ids, x_all, mines, other_core(mines), part)
    sub, cols = part.shape[-2:]
    got = lax.all_to_all(part.reshape(NZH * NZL * NY, sub, cols), ("zh", "zl", "y"), 0, 0, tiled=True)
    got = got.reshape(NZH * NZL, NY, sub, cols)
    piece = jnp.sum(got.astype(jnp.float32), axis=0).astype(jnp.bfloat16)
    line = jnp.stack([piece] + [shift(piece, "zl", NZL, s) for s in range(1, NZL)])
    pieces = [line] + [shift(line, "x", NX, s) for s in range(1, NX)]
    return finish(ids, pieces)


def solution(mesh):
    fine = Mesh(mesh.devices.reshape(NX, NZL, NZH, NY, NC), AXES)
    rows = P(AXES, None)
    out = P(("zh", "y", "c"), None)
    return jax.shard_map(
        shards,
        mesh=fine,
        in_specs=(rows, rows, rows, rows, rows, P(("x", "zl"), None), P()),
        out_specs=(out, out, out),
        check_vma=False,
    )
```

```python
import functools
import math

import jax
import jax.numpy as jnp
from jax import lax
from jax.experimental import pallas as pl
from jax.experimental.pallas import tpu as pltpu
from jax.sharding import Mesh, PartitionSpec as P

HEAD = 128
KV_HEADS = 4
HALF = 64
SPANS = 32
SEQ = 2048
NX, NZL, NZH, NY, NC = 4, 4, 2, 4, 2
ROWS = 128
OWN = ROWS * NY * NC
FEATS = 256
SCALE = 1.0 / math.sqrt(HEAD)
LOG2E = math.log2(math.e)
TILE = 256
VMEM = 60 * 1024 * 1024
AXES = ("x", "zl", "zh", "y", "c")


def nt(a, b):
    return lax.dot_general(a, b, (((1,), (1,)), ((), ())), preferred_element_type=jnp.float32)


def tn(a, b):
    return lax.dot_general(a, b, (((0,), (0,)), ((), ())), preferred_element_type=jnp.float32)


def nn(a, b):
    return lax.dot_general(a, b, (((1,), (0,)), ((), ())), preferred_element_type=jnp.float32)


def cost(us):
    return pl.CostEstimate(flops=us * 1_000_000_000, bytes_accessed=us * 2_000_000, transcendentals=0)


def attention_kernel(ids, span, lens, own, kv, kv_got, dq_ref, keep_ref, give_ref, ks, vs, dk, dv):
    zh, core = ids[0], ids[1]
    blocks = OWN // HALF
    side = zh + core - 2 * zh * core
    for part, first in ((kv, side * blocks), (kv_got, (1 - side) * blocks)):
        for j in range(blocks):
            rows = slice((j % 2) * HALF, (j % 2) * HALF + HALF)
            at = pl.ds(pl.multiple_of(span[first + j] * HALF, HALF), HALF)
            ks[at, :] = part[j // 2, rows, :HEAD]
            vs[at, :] = part[j // 2, rows, HEAD:]
    dk[...] = jnp.zeros_like(dk)
    dv[...] = jnp.zeros_like(dv)
    ends = []
    total = jnp.int32(0)
    for d in range(lens.shape[1]):
        total = total + lens[0, d]
        ends.append(total)
    lane = lax.broadcasted_iota(jnp.int32, (1, 2 * HALF), 1) % HALF

    def block(j, carry):
        first = span[zh * blocks + j] * HALF
        low = jnp.int32(0)
        for e in ends:
            low = jnp.where(e <= first, e, low)
        high = pl.cdiv(first + HALF, 2 * HALF) * (2 * HALF)
        tiles = pl.cdiv(high - low, TILE)
        half, part = j // 2, pl.multiple_of((j % 2) * HALF, HALF)
        q = jnp.concatenate(
            [own[half, pl.ds(part, HALF), :HEAD], own[half, pl.ds(part, HALF), HEAD : 2 * HEAD]], axis=0
        )
        do = jnp.concatenate(
            [own[half, pl.ds(part, HALF), 2 * HEAD : 3 * HEAD], own[half, pl.ds(part, HALF), 3 * HEAD : 4 * HEAD]],
            axis=0,
        )
        pos = first + lane
        doc = jnp.zeros_like(pos)
        for e in ends:
            doc = jnp.where(e <= pos, e, doc)

        def work(n):
            keys = n * TILE
            start = pl.multiple_of(jnp.maximum(high - keys, 0), 2 * HALF)
            at = pl.ds(start, keys)
            k, v = ks[at, :], vs[at, :]
            row = lax.broadcasted_iota(jnp.int32, (keys, 2 * HALF), 0)
            seen = (row >= doc - start) & (row <= pos - start)
            s = jnp.where(seen, nt(k, q), -1e30)
            top = jnp.max(s, axis=0, keepdims=True)
            p = jnp.exp2((s - top) * (SCALE * LOG2E))
            p = p * (1.0 / jnp.sum(p, axis=0, keepdims=True))
            dp = nt(v, do)
            delta = jnp.sum(p * dp, axis=0, keepdims=True)
            ds = (p * (dp - delta)).astype(jnp.bfloat16)
            dv[at, :] += nn(p.astype(jnp.bfloat16), do)
            dk[at, :] += nn(ds, q)
            g = (tn(ds, k) * SCALE).astype(jnp.bfloat16)
            out = pl.ds(pl.multiple_of(j * HALF, HALF), HALF)
            dq_ref[out, :HEAD] = g[:HALF]
            dq_ref[out, HEAD:] = g[HALF:]

        for n in range(1, 6):
            pl.when(tiles == n)(functools.partial(work, n))
        return carry

    lax.fori_loop(0, blocks, block, 0)
    for which, a_ref, b_ref in ((0, keep_ref, give_ref), (1, give_ref, keep_ref)):

        @pl.when(core == which)
        def _(a_ref=a_ref, b_ref=b_ref):
            for j in range(blocks):
                for side, base in ((zh, 0), (1 - zh, OWN)):
                    at = pl.ds(pl.multiple_of(span[side * blocks + j] * HALF, HALF), HALF)
                    to = slice(base + j * HALF, base + (j + 1) * HALF)
                    a_ref[to, :] = (dk[at, :] * SCALE).astype(jnp.bfloat16)
                    b_ref[to, :] = dv[at, :].astype(jnp.bfloat16)


def attention(ids, span, lens, own, kv, kv_got):
    smem = pl.BlockSpec(memory_space=pltpu.SMEM)
    vmem = pl.BlockSpec(memory_space=pltpu.VMEM)
    return pl.pallas_call(
        attention_kernel,
        out_shape=(
            jax.ShapeDtypeStruct((OWN, 2 * HEAD), jnp.bfloat16),
            jax.ShapeDtypeStruct((SEQ, HEAD), jnp.bfloat16),
            jax.ShapeDtypeStruct((SEQ, HEAD), jnp.bfloat16),
        ),
        in_specs=[smem, smem, smem, vmem, vmem, vmem],
        out_specs=(vmem, vmem, vmem),
        cost_estimate=cost(14),
        scratch_shapes=[
            pltpu.VMEM((SEQ, HEAD), jnp.bfloat16),
            pltpu.VMEM((SEQ, HEAD), jnp.bfloat16),
            pltpu.VMEM((SEQ, HEAD), jnp.float32),
            pltpu.VMEM((SEQ, HEAD), jnp.float32),
        ],
        compiler_params=pltpu.CompilerParams(vmem_limit_bytes=VMEM),
        name="attention_backward",
    )(ids, span, lens, own, kv, kv_got)


def turn_kernel(ids, x_ref, keep, give, turned):
    core, x = ids[1], ids[2]
    rows = FEATS // NX
    for out, which in ((keep, core), (give, 1 - core)):
        for i in range(NZH * NY):
            turned[i % 2] = x_ref[:, pl.ds(pl.multiple_of((2 * i + which) * FEATS, FEATS), FEATS)].T
            for s in range(NX):
                at = pl.ds(pl.multiple_of(lax.rem(x + s, NX) * rows, rows), rows)
                out[s, i * rows : (i + 1) * rows, :] = turned[i % 2, at, :]


def turn(ids, x):
    smem = pl.BlockSpec(memory_space=pltpu.SMEM)
    vmem = pl.BlockSpec(memory_space=pltpu.VMEM)
    shape = jax.ShapeDtypeStruct((NX, NZH * NY * FEATS // NX, ROWS), jnp.bfloat16)
    return pl.pallas_call(
        turn_kernel,
        out_shape=(shape, shape),
        in_specs=[smem, vmem],
        out_specs=(vmem, vmem),
        scratch_shapes=[pltpu.VMEM((2, FEATS, ROWS), jnp.bfloat16)],
        compiler_params=pltpu.CompilerParams(vmem_limit_bytes=VMEM),
        name="turn",
    )(ids, x)


def weight_kernel(joined, ids, *refs):
    pieces, mine, got, out, g = refs[:8], refs[8 : 8 + NX], refs[8 + NX : 8 + 2 * NX], refs[-2], refs[-1]
    core, y = ids[1], ids[3]
    width = mine[0].shape[1]
    for i, s in enumerate((0, -1, 1, 2)):
        base = lax.rem(y + s + NY, NY) * (NC * ROWS)
        for t in range(NX):
            for half, which in enumerate((core, 1 - core)):
                at = pl.ds(pl.multiple_of(base + which * ROWS, ROWS), ROWS)
                to = slice((2 * t + half) * ROWS, (2 * t + half + 1) * ROWS)
                g[i, to, :width] = mine[t][at, :]
                g[i, to, width:] = got[t][at, :]
    sub = FEATS // (NX * NZL)
    first = 0
    if joined:
        before = refs[8 + 2 * NX]
        first = before.shape[-1]
        out[:, :, :, :, :first] = before[...]
    for zh in range(NZH):
        total = jnp.zeros((FEATS, 2 * width), jnp.float32)
        for i in range(NY):
            total += nn(pieces[4 * zh + i][...], g[i])
        total = total.astype(jnp.bfloat16)
        for y_to in range(NY):
            for zl in range(NZL):
                row = (y_to * NZL + zl) * sub
                out[zh, zl, y_to, :, first : first + 2 * width] = total[row : row + sub]


def weight_term(ids, xs, mine, got, before=None):
    width = mine[0].shape[1]
    cols = 2 * width + (before.shape[-1] if before is not None else 0)
    vmem = pl.BlockSpec(memory_space=pltpu.VMEM)
    more = [] if before is None else [before]
    return pl.pallas_call(
        functools.partial(weight_kernel, before is not None),
        out_shape=jax.ShapeDtypeStruct((NZH, NZL, NY, FEATS // (NX * NZL), cols), jnp.bfloat16),
        in_specs=[pl.BlockSpec(memory_space=pltpu.SMEM)] + [vmem] * (len(xs) + 2 * NX + len(more)),
        out_specs=vmem,
        scratch_shapes=[pltpu.VMEM((NY, OWN, 2 * width), jnp.bfloat16)],
        compiler_params=pltpu.CompilerParams(vmem_limit_bytes=VMEM),
        cost_estimate=cost(5),
        name="weight_term",
    )(ids, *xs, *mine, *got, *more)


def finish_kernel(ids, *refs):
    pieces, (q_ref, k_ref, v_ref) = refs[:NX], refs[NX:]
    core, x, zl = ids[1], ids[2], ids[4]
    sub = FEATS // (NX * NZL)
    for sx in range(NX):
        for sz in range(NZL):
            row = lax.rem(x - sx + NX, NX) * (FEATS // NX) + lax.rem(zl - sz + NZL, NZL) * sub
            at = pl.ds(pl.multiple_of(row, sub), sub)
            for y in range(NY):
                got = pieces[sx].at[sz, y]
                for i, which in enumerate((core, 1 - core)):
                    src = pl.ds(pl.multiple_of(which * 2 * HEAD, 2 * HEAD), 2 * HEAD)
                    to = slice((2 * y + i) * 2 * HEAD, (2 * y + i + 1) * 2 * HEAD)
                    q_ref[at, to] = got[:, src].astype(jnp.float32)
                    src = pl.ds(pl.multiple_of((4 + which) * HEAD, HEAD), HEAD)
                    (k_ref, v_ref)[i][at, y * HEAD : (y + 1) * HEAD] = got[:, src].astype(jnp.float32)


def finish(ids, pieces):
    smem = pl.BlockSpec(memory_space=pltpu.SMEM)
    vmem = pl.BlockSpec(memory_space=pltpu.VMEM)
    cols = KV_HEADS * HEAD
    return pl.pallas_call(
        finish_kernel,
        out_shape=(
            jax.ShapeDtypeStruct((FEATS, NY * cols), jnp.float32),
            jax.ShapeDtypeStruct((FEATS, cols), jnp.float32),
            jax.ShapeDtypeStruct((FEATS, cols), jnp.float32),
        ),
        in_specs=[smem] + [vmem] * len(pieces),
        out_specs=(vmem, vmem, vmem),
        compiler_params=pltpu.CompilerParams(vmem_limit_bytes=VMEM),
        name="finish",
    )(ids, *pieces)


def shift(value, axis, n, s):
    return lax.ppermute(value, axis, [(i, (i + s) % n) for i in range(n)])


def by_head(value, copies):
    return jnp.broadcast_to(value.reshape(ROWS, KV_HEADS, 1, HEAD), (ROWS, KV_HEADS, copies, HEAD)).reshape(
        ROWS, KV_HEADS * copies, HEAD
    )


def gather_x(value):
    return [value] + [shift(value, "x", NX, s) for s in range(1, NX)]


def other_core(values):
    rest = shift(jnp.concatenate(values[1:], axis=0), "c", NC, 1)
    n = values[0].shape[0]
    return [shift(values[0], "c", NC, 1)] + [rest[i * n : (i + 1) * n] for i in range(len(values) - 1)]


def shards(x, q, k, v, do, lens, span):
    ids = jnp.stack([lax.axis_index(a) for a in ("zh", "c", "x", "y", "zl")]).astype(jnp.int32)
    groups = NY * NC
    kv_rows = jnp.concatenate([k, v], axis=1)
    send = jnp.concatenate(
        [q.reshape(ROWS, groups, 2 * HEAD), do.reshape(ROWS, groups, 2 * HEAD)], axis=2
    ).transpose(1, 0, 2)
    kv_rows, x, send = lax.optimization_barrier((kv_rows, x, send))
    own = lax.all_to_all(send, ("y", "c"), 0, 0, tiled=True)
    far = shift(kv_rows, "zh", NZH, 1)

    keep, give = turn(ids, x)
    pair = jnp.concatenate([keep, shift(give, "c", NC, 1)], axis=2)
    quarters = [pair[0]] + [shift(pair[t], "x", NX, t) for t in range(1, NX)]
    send = jnp.stack([kv_rows, far]).reshape(NC, ROWS, 2, KV_HEADS, HEAD)
    send = send.transpose(3, 0, 1, 2, 4).reshape(groups, ROWS, 2 * HEAD)
    own, send, *quarters = lax.optimization_barrier((own, send, *quarters))
    xa, xb = (
        jnp.concatenate([t[h * FEATS : (h + 1) * FEATS] for t in quarters], axis=1) for h in range(NZH)
    )
    kv = lax.all_to_all(send, ("y", "c"), 0, 0, tiled=True)
    kv_got = shift(kv, "c", NC, 1)

    xa_up, xb_up = shift(xa, "y", NY, 1), shift(xb, "y", NY, 1)
    xa_down, xb_down = shift(xa, "y", NY, -1), shift(xb, "y", NY, -1)
    dq, kept, given = attention(ids, span, lens, own, kv, kv_got)
    dq, kept, given, xa_up, xb_down, xa_down, xb_up = lax.optimization_barrier(
        (dq, kept, given, xa_up, xb_down, xa_down, xb_up)
    )
    dqs = gather_x(dq)
    both = kept.astype(jnp.float32) + shift(given, "c", NC, 1).astype(jnp.float32)
    both, xa_up, xb_down = lax.optimization_barrier((both, xa_up, xb_down))
    xa_far, xb_far = shift(xa_up, "y", NY, 1), shift(xb_down, "y", NY, -1)
    got = shift(both[OWN:].astype(jnp.bfloat16), "zh", NZH, 1)
    got, *dqs = lax.optimization_barrier((got, *dqs))
    xa_far, xb_far, *dqs = lax.optimization_barrier((xa_far, xb_far, *dqs))
    x_all = [xa, xa_up, xa_down, xa_far, xb, xb_up, xb_down, xb_far]
    mine = (both[:OWN] + got.astype(jnp.float32)).astype(jnp.bfloat16)
    mines = gather_x(mine)
    part = weight_term(ids, x_all, dqs, other_core(dqs))
    part, *mines = lax.optimization_barrier((part, *mines))
    part = weight_term(ids, x_all, mines, other_core(mines), part)
    sub, cols = part.shape[-2:]
    got = lax.all_to_all(part.reshape(NZH * NZL * NY, sub, cols), ("zh", "zl", "y"), 0, 0, tiled=True)
    got = got.reshape(NZH * NZL, NY, sub, cols)
    piece = jnp.sum(got.astype(jnp.float32), axis=0).astype(jnp.bfloat16)
    line = jnp.stack([piece] + [shift(piece, "zl", NZL, s) for s in range(1, NZL)])
    pieces = [line] + [shift(line, "x", NX, s) for s in range(1, NX)]
    return finish(ids, pieces)


def solution(mesh):
    fine = Mesh(mesh.devices.reshape(NX, NZL, NZH, NY, NC), AXES)
    rows = P(AXES, None)
    out = P(("zh", "y", "c"), None)
    return jax.shard_map(
        shards,
        mesh=fine,
        in_specs=(rows, rows, rows, rows, rows, P(("x", "zl"), None), P()),
        out_specs=(out, out, out),
        check_vma=False,
    )
```

```python
import functools
import math

import jax
import jax.numpy as jnp
from jax import lax
from jax.experimental import pallas as pl
from jax.experimental.pallas import tpu as pltpu
from jax.sharding import Mesh, PartitionSpec as P

HEAD = 128
KV_HEADS = 4
HALF = 64
SPANS = 32
SEQ = 2048
NX, NZL, NZH, NY, NC = 4, 4, 2, 4, 2
ROWS = 128
OWN = ROWS * NY * NC
FEATS = 256
SCALE = 1.0 / math.sqrt(HEAD)
LOG2E = math.log2(math.e)
TILE = 256
VMEM = 60 * 1024 * 1024
AXES = ("x", "zl", "zh", "y", "c")


def nt(a, b):
    return lax.dot_general(a, b, (((1,), (1,)), ((), ())), preferred_element_type=jnp.float32)


def tn(a, b):
    return lax.dot_general(a, b, (((0,), (0,)), ((), ())), preferred_element_type=jnp.float32)


def nn(a, b):
    return lax.dot_general(a, b, (((1,), (0,)), ((), ())), preferred_element_type=jnp.float32)


def cost(us):
    return pl.CostEstimate(flops=us * 1_000_000_000, bytes_accessed=us * 2_000_000, transcendentals=0)


def attention_kernel(ids, span, lens, own, kv, kv_got, dq_ref, keep_ref, give_ref, ks, vs, dk, dv):
    zh, core = ids[0], ids[1]
    blocks = OWN // HALF
    side = zh + core - 2 * zh * core
    for part, first in ((kv, side * blocks), (kv_got, (1 - side) * blocks)):
        for j in range(blocks):
            rows = slice((j % 2) * HALF, (j % 2) * HALF + HALF)
            at = pl.ds(pl.multiple_of(span[first + j] * HALF, HALF), HALF)
            ks[at, :] = part[j // 2, rows, :HEAD]
            vs[at, :] = part[j // 2, rows, HEAD:]
    dk[...] = jnp.zeros_like(dk)
    dv[...] = jnp.zeros_like(dv)
    ends = []
    total = jnp.int32(0)
    for d in range(lens.shape[1]):
        total = total + lens[0, d]
        ends.append(total)
    lane = lax.broadcasted_iota(jnp.int32, (1, 2 * HALF), 1) % HALF

    def block(j, carry):
        first = span[zh * blocks + j] * HALF
        low = jnp.int32(0)
        for e in ends:
            low = jnp.where(e <= first, e, low)
        high = pl.cdiv(first + HALF, 2 * HALF) * (2 * HALF)
        tiles = pl.cdiv(high - low, TILE)
        half, part = j // 2, pl.multiple_of((j % 2) * HALF, HALF)
        q = jnp.concatenate(
            [own[half, pl.ds(part, HALF), :HEAD], own[half, pl.ds(part, HALF), HEAD : 2 * HEAD]], axis=0
        )
        do = jnp.concatenate(
            [own[half, pl.ds(part, HALF), 2 * HEAD : 3 * HEAD], own[half, pl.ds(part, HALF), 3 * HEAD : 4 * HEAD]],
            axis=0,
        )
        pos = first + lane
        doc = jnp.zeros_like(pos)
        for e in ends:
            doc = jnp.where(e <= pos, e, doc)

        def work(n):
            keys = n * TILE
            start = pl.multiple_of(jnp.maximum(high - keys, 0), 2 * HALF)
            at = pl.ds(start, keys)
            k, v = ks[at, :], vs[at, :]
            row = lax.broadcasted_iota(jnp.int32, (keys, 2 * HALF), 0)
            seen = (row >= doc - start) & (row <= pos - start)
            s = jnp.where(seen, nt(k, q), -1e30)
            top = jnp.max(s, axis=0, keepdims=True)
            p = jnp.exp2((s - top) * (SCALE * LOG2E))
            p = p * (1.0 / jnp.sum(p, axis=0, keepdims=True))
            dp = nt(v, do)
            delta = jnp.sum(p * dp, axis=0, keepdims=True)
            ds = (p * (dp - delta)).astype(jnp.bfloat16)
            dv[at, :] += nn(p.astype(jnp.bfloat16), do)
            dk[at, :] += nn(ds, q)
            g = (tn(ds, k) * SCALE).astype(jnp.bfloat16)
            out = pl.ds(pl.multiple_of(j * HALF, HALF), HALF)
            dq_ref[out, :HEAD] = g[:HALF]
            dq_ref[out, HEAD:] = g[HALF:]

        for n in range(1, 6):
            pl.when(tiles == n)(functools.partial(work, n))
        return carry

    lax.fori_loop(0, blocks, block, 0)
    for which, a_ref, b_ref in ((0, keep_ref, give_ref), (1, give_ref, keep_ref)):

        @pl.when(core == which)
        def _(a_ref=a_ref, b_ref=b_ref):
            for j in range(blocks):
                for side, base in ((zh, 0), (1 - zh, OWN)):
                    at = pl.ds(pl.multiple_of(span[side * blocks + j] * HALF, HALF), HALF)
                    to = slice(base + j * HALF, base + (j + 1) * HALF)
                    a_ref[to, :] = (dk[at, :] * SCALE).astype(jnp.bfloat16)
                    b_ref[to, :] = dv[at, :].astype(jnp.bfloat16)


def attention(ids, span, lens, own, kv, kv_got):
    smem = pl.BlockSpec(memory_space=pltpu.SMEM)
    vmem = pl.BlockSpec(memory_space=pltpu.VMEM)
    return pl.pallas_call(
        attention_kernel,
        out_shape=(
            jax.ShapeDtypeStruct((OWN, 2 * HEAD), jnp.bfloat16),
            jax.ShapeDtypeStruct((SEQ, HEAD), jnp.bfloat16),
            jax.ShapeDtypeStruct((SEQ, HEAD), jnp.bfloat16),
        ),
        in_specs=[smem, smem, smem, vmem, vmem, vmem],
        out_specs=(vmem, vmem, vmem),
        cost_estimate=cost(14),
        scratch_shapes=[
            pltpu.VMEM((SEQ, HEAD), jnp.bfloat16),
            pltpu.VMEM((SEQ, HEAD), jnp.bfloat16),
            pltpu.VMEM((SEQ, HEAD), jnp.float32),
            pltpu.VMEM((SEQ, HEAD), jnp.float32),
        ],
        compiler_params=pltpu.CompilerParams(vmem_limit_bytes=VMEM),
        name="attention_backward",
    )(ids, span, lens, own, kv, kv_got)


def turn_kernel(ids, x_ref, keep, give, turned):
    core, x = ids[1], ids[2]
    rows = FEATS // NX
    for out, which in ((keep, core), (give, 1 - core)):
        for i in range(NZH * NY):
            turned[i % 2] = x_ref[:, pl.ds(pl.multiple_of((2 * i + which) * FEATS, FEATS), FEATS)].T
            for s in range(NX):
                at = pl.ds(pl.multiple_of(lax.rem(x + s, NX) * rows, rows), rows)
                out[s, i * rows : (i + 1) * rows, :] = turned[i % 2, at, :]


def turn(ids, x):
    smem = pl.BlockSpec(memory_space=pltpu.SMEM)
    vmem = pl.BlockSpec(memory_space=pltpu.VMEM)
    shape = jax.ShapeDtypeStruct((NX, NZH * NY * FEATS // NX, ROWS), jnp.bfloat16)
    return pl.pallas_call(
        turn_kernel,
        out_shape=(shape, shape),
        in_specs=[smem, vmem],
        out_specs=(vmem, vmem),
        scratch_shapes=[pltpu.VMEM((2, FEATS, ROWS), jnp.bfloat16)],
        compiler_params=pltpu.CompilerParams(vmem_limit_bytes=VMEM),
        name="turn",
    )(ids, x)


def weight_kernel(joined, ids, *refs):
    pieces, mine, got, out, g = refs[:8], refs[8 : 8 + NX], refs[8 + NX : 8 + 2 * NX], refs[-2], refs[-1]
    core, y = ids[1], ids[3]
    width = mine[0].shape[1]
    for i, s in enumerate((0, -1, 1, 2)):
        base = lax.rem(y + s + NY, NY) * (NC * ROWS)
        for t in range(NX):
            for half, which in enumerate((core, 1 - core)):
                at = pl.ds(pl.multiple_of(base + which * ROWS, ROWS), ROWS)
                to = slice((2 * t + half) * ROWS, (2 * t + half + 1) * ROWS)
                g[i, to, :width] = mine[t][at, :]
                g[i, to, width:] = got[t][at, :]
    sub = FEATS // (NX * NZL)
    first = 0
    if joined:
        before = refs[8 + 2 * NX]
        first = before.shape[-1]
        out[:, :, :, :, :first] = before[...]
    for zh in range(NZH):
        total = jnp.zeros((FEATS, 2 * width), jnp.float32)
        for i in range(NY):
            total += nn(pieces[4 * zh + i][...], g[i])
        total = total.astype(jnp.bfloat16)
        for y_to in range(NY):
            for zl in range(NZL):
                row = (y_to * NZL + zl) * sub
                out[zh, zl, y_to, :, first : first + 2 * width] = total[row : row + sub]


def weight_term(ids, xs, mine, got, before=None):
    width = mine[0].shape[1]
    cols = 2 * width + (before.shape[-1] if before is not None else 0)
    vmem = pl.BlockSpec(memory_space=pltpu.VMEM)
    more = [] if before is None else [before]
    return pl.pallas_call(
        functools.partial(weight_kernel, before is not None),
        out_shape=jax.ShapeDtypeStruct((NZH, NZL, NY, FEATS // (NX * NZL), cols), jnp.bfloat16),
        in_specs=[pl.BlockSpec(memory_space=pltpu.SMEM)] + [vmem] * (len(xs) + 2 * NX + len(more)),
        out_specs=vmem,
        scratch_shapes=[pltpu.VMEM((NY, OWN, 2 * width), jnp.bfloat16)],
        compiler_params=pltpu.CompilerParams(vmem_limit_bytes=VMEM),
        cost_estimate=cost(5),
        name="weight_term",
    )(ids, *xs, *mine, *got, *more)


def finish_kernel(ids, *refs):
    pieces, (q_ref, k_ref, v_ref) = refs[:NX], refs[NX:]
    core, x, zl = ids[1], ids[2], ids[4]
    sub = FEATS // (NX * NZL)
    for sx in range(NX):
        for sz in range(NZL):
            row = lax.rem(x - sx + NX, NX) * (FEATS // NX) + lax.rem(zl - sz + NZL, NZL) * sub
            at = pl.ds(pl.multiple_of(row, sub), sub)
            for y in range(NY):
                got = pieces[sx].at[sz, y]
                for i, which in enumerate((core, 1 - core)):
                    src = pl.ds(pl.multiple_of(which * 2 * HEAD, 2 * HEAD), 2 * HEAD)
                    to = slice((2 * y + i) * 2 * HEAD, (2 * y + i + 1) * 2 * HEAD)
                    q_ref[at, to] = got[:, src].astype(jnp.float32)
                    src = pl.ds(pl.multiple_of((4 + which) * HEAD, HEAD), HEAD)
                    (k_ref, v_ref)[i][at, y * HEAD : (y + 1) * HEAD] = got[:, src].astype(jnp.float32)


def finish(ids, pieces):
    smem = pl.BlockSpec(memory_space=pltpu.SMEM)
    vmem = pl.BlockSpec(memory_space=pltpu.VMEM)
    cols = KV_HEADS * HEAD
    return pl.pallas_call(
        finish_kernel,
        out_shape=(
            jax.ShapeDtypeStruct((FEATS, NY * cols), jnp.float32),
            jax.ShapeDtypeStruct((FEATS, cols), jnp.float32),
            jax.ShapeDtypeStruct((FEATS, cols), jnp.float32),
        ),
        in_specs=[smem] + [vmem] * len(pieces),
        out_specs=(vmem, vmem, vmem),
        compiler_params=pltpu.CompilerParams(vmem_limit_bytes=VMEM),
        name="finish",
    )(ids, *pieces)


def shift(value, axis, n, s):
    return lax.ppermute(value, axis, [(i, (i + s) % n) for i in range(n)])


def by_head(value, copies):
    return jnp.broadcast_to(value.reshape(ROWS, KV_HEADS, 1, HEAD), (ROWS, KV_HEADS, copies, HEAD)).reshape(
        ROWS, KV_HEADS * copies, HEAD
    )


def gather_x(value):
    return [value] + [shift(value, "x", NX, s) for s in range(1, NX)]


def other_core(values):
    rest = shift(jnp.concatenate(values[1:], axis=0), "c", NC, 1)
    n = values[0].shape[0]
    return [shift(values[0], "c", NC, 1)] + [rest[i * n : (i + 1) * n] for i in range(len(values) - 1)]


def shards(x, q, k, v, do, lens, span):
    ids = jnp.stack([lax.axis_index(a) for a in ("zh", "c", "x", "y", "zl")]).astype(jnp.int32)
    groups = NY * NC
    kv_rows = jnp.concatenate([k, v], axis=1)
    send = jnp.concatenate(
        [q.reshape(ROWS, groups, 2 * HEAD), do.reshape(ROWS, groups, 2 * HEAD)], axis=2
    ).transpose(1, 0, 2)
    kv_rows, x, send = lax.optimization_barrier((kv_rows, x, send))
    own = lax.all_to_all(send, ("y", "c"), 0, 0, tiled=True)
    far = shift(kv_rows, "zh", NZH, 1)

    keep, give = turn(ids, x)
    pair = jnp.concatenate([keep, shift(give, "c", NC, 1)], axis=2)
    quarters = [pair[0]] + [shift(pair[t], "x", NX, t) for t in range(1, NX)]
    send = jnp.stack([kv_rows, far]).reshape(NC, ROWS, 2, KV_HEADS, HEAD)
    send = send.transpose(3, 0, 1, 2, 4).reshape(groups, ROWS, 2 * HEAD)
    own, send, *quarters = lax.optimization_barrier((own, send, *quarters))
    xa, xb = (
        jnp.concatenate([t[h * FEATS : (h + 1) * FEATS] for t in quarters], axis=1) for h in range(NZH)
    )
    kv = lax.all_to_all(send, ("y", "c"), 0, 0, tiled=True)
    kv_got = shift(kv, "c", NC, 1)

    xa_up, xb_up = shift(xa, "y", NY, 1), shift(xb, "y", NY, 1)
    xa_down, xb_down = shift(xa, "y", NY, -1), shift(xb, "y", NY, -1)
    dq, kept, given = attention(ids, span, lens, own, kv, kv_got)
    dq, kept, given, xa_up, xb_down, xa_down, xb_up = lax.optimization_barrier(
        (dq, kept, given, xa_up, xb_down, xa_down, xb_up)
    )
    dqs = gather_x(dq)
    both = kept.astype(jnp.float32) + shift(given, "c", NC, 1).astype(jnp.float32)
    both, xa_up = lax.optimization_barrier((both, xa_up))
    xa_far = shift(xa_up, "y", NY, 1)
    got = shift(both[OWN:].astype(jnp.bfloat16), "zh", NZH, 1)
    got, xb_down, *dqs = lax.optimization_barrier((got, xb_down, *dqs))
    xb_far = shift(xb_down, "y", NY, -1)
    xa_far, *dqs = lax.optimization_barrier((xa_far, *dqs))
    x_all = [xa, xa_up, xa_down, xa_far, xb, xb_up, xb_down, xb_far]
    mine = (both[:OWN] + got.astype(jnp.float32)).astype(jnp.bfloat16)
    mines = gather_x(mine)
    part = weight_term(ids, x_all, dqs, other_core(dqs))
    part, *mines = lax.optimization_barrier((part, *mines))
    part = weight_term(ids, x_all, mines, other_core(mines), part)
    sub, cols = part.shape[-2:]
    got = lax.all_to_all(part.reshape(NZH * NZL * NY, sub, cols), ("zh", "zl", "y"), 0, 0, tiled=True)
    got = got.reshape(NZH * NZL, NY, sub, cols)
    piece = jnp.sum(got.astype(jnp.float32), axis=0).astype(jnp.bfloat16)
    line = jnp.stack([piece] + [shift(piece, "zl", NZL, s) for s in range(1, NZL)])
    pieces = [line] + [shift(line, "x", NX, s) for s in range(1, NX)]
    return finish(ids, pieces)


def solution(mesh):
    fine = Mesh(mesh.devices.reshape(NX, NZL, NZH, NY, NC), AXES)
    rows = P(AXES, None)
    out = P(("zh", "y", "c"), None)
    return jax.shard_map(
        shards,
        mesh=fine,
        in_specs=(rows, rows, rows, rows, rows, P(("x", "zl"), None), P()),
        out_specs=(out, out, out),
        check_vma=False,
    )
```

```python
import functools
import math

import jax
import jax.numpy as jnp
from jax import lax
from jax.experimental import pallas as pl
from jax.experimental.pallas import tpu as pltpu
from jax.sharding import Mesh, PartitionSpec as P

HEAD = 128
KV_HEADS = 4
HALF = 64
SPANS = 32
SEQ = 2048
NX, NZL, NZH, NY, NC = 4, 4, 2, 4, 2
ROWS = 128
OWN = ROWS * NY * NC
FEATS = 256
SCALE = 1.0 / math.sqrt(HEAD)
LOG2E = math.log2(math.e)
TILE = 256
VMEM = 60 * 1024 * 1024
AXES = ("x", "zl", "zh", "y", "c")


def nt(a, b):
    return lax.dot_general(a, b, (((1,), (1,)), ((), ())), preferred_element_type=jnp.float32)


def tn(a, b):
    return lax.dot_general(a, b, (((0,), (0,)), ((), ())), preferred_element_type=jnp.float32)


def nn(a, b):
    return lax.dot_general(a, b, (((1,), (0,)), ((), ())), preferred_element_type=jnp.float32)


def cost(us):
    return pl.CostEstimate(flops=us * 1_000_000_000, bytes_accessed=us * 2_000_000, transcendentals=0)


def attention_kernel(ids, span, lens, own, kv, kv_got, dq_ref, keep_ref, give_ref, ks, vs, dk, dv):
    zh, core = ids[0], ids[1]
    blocks = OWN // HALF
    side = zh + core - 2 * zh * core
    for part, first in ((kv, side * blocks), (kv_got, (1 - side) * blocks)):
        for j in range(blocks):
            rows = slice((j % 2) * HALF, (j % 2) * HALF + HALF)
            at = pl.ds(pl.multiple_of(span[first + j] * HALF, HALF), HALF)
            ks[at, :] = part[j // 2, rows, :HEAD]
            vs[at, :] = part[j // 2, rows, HEAD:]
    dk[...] = jnp.zeros_like(dk)
    dv[...] = jnp.zeros_like(dv)
    ends = []
    total = jnp.int32(0)
    for d in range(lens.shape[1]):
        total = total + lens[0, d]
        ends.append(total)
    lane = lax.broadcasted_iota(jnp.int32, (1, 2 * HALF), 1) % HALF

    def block(j, carry):
        first = span[zh * blocks + j] * HALF
        low = jnp.int32(0)
        for e in ends:
            low = jnp.where(e <= first, e, low)
        high = pl.cdiv(first + HALF, 2 * HALF) * (2 * HALF)
        tiles = pl.cdiv(high - low, TILE)
        half, part = j // 2, pl.multiple_of((j % 2) * HALF, HALF)
        q = jnp.concatenate(
            [own[half, pl.ds(part, HALF), :HEAD], own[half, pl.ds(part, HALF), HEAD : 2 * HEAD]], axis=0
        )
        do = jnp.concatenate(
            [own[half, pl.ds(part, HALF), 2 * HEAD : 3 * HEAD], own[half, pl.ds(part, HALF), 3 * HEAD : 4 * HEAD]],
            axis=0,
        )
        pos = first + lane
        doc = jnp.zeros_like(pos)
        for e in ends:
            doc = jnp.where(e <= pos, e, doc)

        def work(n):
            keys = n * TILE
            start = pl.multiple_of(jnp.maximum(high - keys, 0), 2 * HALF)
            at = pl.ds(start, keys)
            k, v = ks[at, :], vs[at, :]
            row = lax.broadcasted_iota(jnp.int32, (keys, 2 * HALF), 0)
            seen = (row >= doc - start) & (row <= pos - start)
            s = jnp.where(seen, nt(k, q), -1e30)
            top = jnp.max(s, axis=0, keepdims=True)
            p = jnp.exp2((s - top) * (SCALE * LOG2E))
            p = p * (1.0 / jnp.sum(p, axis=0, keepdims=True))
            dp = nt(v, do)
            delta = jnp.sum(p * dp, axis=0, keepdims=True)
            ds = (p * (dp - delta)).astype(jnp.bfloat16)
            dv[at, :] += nn(p.astype(jnp.bfloat16), do)
            dk[at, :] += nn(ds, q)
            g = (tn(ds, k) * SCALE).astype(jnp.bfloat16)
            out = pl.ds(pl.multiple_of(j * HALF, HALF), HALF)
            dq_ref[out, :HEAD] = g[:HALF]
            dq_ref[out, HEAD:] = g[HALF:]

        for n in range(1, 6):
            pl.when(tiles == n)(functools.partial(work, n))
        return carry

    lax.fori_loop(0, blocks, block, 0)
    for which, a_ref, b_ref in ((0, keep_ref, give_ref), (1, give_ref, keep_ref)):

        @pl.when(core == which)
        def _(a_ref=a_ref, b_ref=b_ref):
            for j in range(blocks):
                for side, base in ((zh, 0), (1 - zh, OWN)):
                    at = pl.ds(pl.multiple_of(span[side * blocks + j] * HALF, HALF), HALF)
                    to = slice(base + j * HALF, base + (j + 1) * HALF)
                    a_ref[to, :] = (dk[at, :] * SCALE).astype(jnp.bfloat16)
                    b_ref[to, :] = dv[at, :].astype(jnp.bfloat16)


def attention(ids, span, lens, own, kv, kv_got):
    smem = pl.BlockSpec(memory_space=pltpu.SMEM)
    vmem = pl.BlockSpec(memory_space=pltpu.VMEM)
    return pl.pallas_call(
        attention_kernel,
        out_shape=(
            jax.ShapeDtypeStruct((OWN, 2 * HEAD), jnp.bfloat16),
            jax.ShapeDtypeStruct((SEQ, HEAD), jnp.bfloat16),
            jax.ShapeDtypeStruct((SEQ, HEAD), jnp.bfloat16),
        ),
        in_specs=[smem, smem, smem, vmem, vmem, vmem],
        out_specs=(vmem, vmem, vmem),
        cost_estimate=cost(14),
        scratch_shapes=[
            pltpu.VMEM((SEQ, HEAD), jnp.bfloat16),
            pltpu.VMEM((SEQ, HEAD), jnp.bfloat16),
            pltpu.VMEM((SEQ, HEAD), jnp.float32),
            pltpu.VMEM((SEQ, HEAD), jnp.float32),
        ],
        compiler_params=pltpu.CompilerParams(vmem_limit_bytes=VMEM),
        name="attention_backward",
    )(ids, span, lens, own, kv, kv_got)


def turn_kernel(ids, x_ref, keep, give, turned):
    core, x = ids[1], ids[2]
    rows = FEATS // NX
    for out, which in ((keep, core), (give, 1 - core)):
        for i in range(NZH * NY):
            turned[i % 2] = x_ref[:, pl.ds(pl.multiple_of((2 * i + which) * FEATS, FEATS), FEATS)].T
            for s in range(NX):
                at = pl.ds(pl.multiple_of(lax.rem(x + s, NX) * rows, rows), rows)
                out[s, i * rows : (i + 1) * rows, :] = turned[i % 2, at, :]


def turn(ids, x):
    smem = pl.BlockSpec(memory_space=pltpu.SMEM)
    vmem = pl.BlockSpec(memory_space=pltpu.VMEM)
    shape = jax.ShapeDtypeStruct((NX, NZH * NY * FEATS // NX, ROWS), jnp.bfloat16)
    return pl.pallas_call(
        turn_kernel,
        out_shape=(shape, shape),
        in_specs=[smem, vmem],
        out_specs=(vmem, vmem),
        scratch_shapes=[pltpu.VMEM((2, FEATS, ROWS), jnp.bfloat16)],
        compiler_params=pltpu.CompilerParams(vmem_limit_bytes=VMEM),
        name="turn",
    )(ids, x)


def weight_kernel(joined, ids, *refs):
    pieces, mine, got, out, g = refs[:8], refs[8 : 8 + NX], refs[8 + NX : 8 + 2 * NX], refs[-2], refs[-1]
    core, y = ids[1], ids[3]
    width = mine[0].shape[1]
    for i, s in enumerate((0, -1, 1, 2)):
        base = lax.rem(y + s + NY, NY) * (NC * ROWS)
        for t in range(NX):
            for half, which in enumerate((core, 1 - core)):
                at = pl.ds(pl.multiple_of(base + which * ROWS, ROWS), ROWS)
                to = slice((2 * t + half) * ROWS, (2 * t + half + 1) * ROWS)
                g[i, to, :width] = mine[t][at, :]
                g[i, to, width:] = got[t][at, :]
    sub = FEATS // (NX * NZL)
    first = 0
    if joined:
        before = refs[8 + 2 * NX]
        first = before.shape[-1]
        out[:, :, :, :, :first] = before[...]
    for zh in range(NZH):
        total = jnp.zeros((FEATS, 2 * width), jnp.float32)
        for i in range(NY):
            total += nn(pieces[4 * zh + i][...], g[i])
        total = total.astype(jnp.bfloat16)
        for y_to in range(NY):
            for zl in range(NZL):
                row = (y_to * NZL + zl) * sub
                out[zh, zl, y_to, :, first : first + 2 * width] = total[row : row + sub]


def weight_term(ids, xs, mine, got, before=None):
    width = mine[0].shape[1]
    cols = 2 * width + (before.shape[-1] if before is not None else 0)
    vmem = pl.BlockSpec(memory_space=pltpu.VMEM)
    more = [] if before is None else [before]
    return pl.pallas_call(
        functools.partial(weight_kernel, before is not None),
        out_shape=jax.ShapeDtypeStruct((NZH, NZL, NY, FEATS // (NX * NZL), cols), jnp.bfloat16),
        in_specs=[pl.BlockSpec(memory_space=pltpu.SMEM)] + [vmem] * (len(xs) + 2 * NX + len(more)),
        out_specs=vmem,
        scratch_shapes=[pltpu.VMEM((NY, OWN, 2 * width), jnp.bfloat16)],
        compiler_params=pltpu.CompilerParams(vmem_limit_bytes=VMEM),
        cost_estimate=cost(5),
        name="weight_term",
    )(ids, *xs, *mine, *got, *more)


def finish_kernel(ids, *refs):
    pieces, (q_ref, k_ref, v_ref) = refs[:NX], refs[NX:]
    core, x, zl = ids[1], ids[2], ids[4]
    sub = FEATS // (NX * NZL)
    for sx in range(NX):
        for sz in range(NZL):
            row = lax.rem(x - sx + NX, NX) * (FEATS // NX) + lax.rem(zl - sz + NZL, NZL) * sub
            at = pl.ds(pl.multiple_of(row, sub), sub)
            for y in range(NY):
                got = pieces[sx].at[sz, y]
                for i, which in enumerate((core, 1 - core)):
                    src = pl.ds(pl.multiple_of(which * 2 * HEAD, 2 * HEAD), 2 * HEAD)
                    to = slice((2 * y + i) * 2 * HEAD, (2 * y + i + 1) * 2 * HEAD)
                    q_ref[at, to] = got[:, src].astype(jnp.float32)
                    src = pl.ds(pl.multiple_of((4 + which) * HEAD, HEAD), HEAD)
                    (k_ref, v_ref)[i][at, y * HEAD : (y + 1) * HEAD] = got[:, src].astype(jnp.float32)


def finish(ids, pieces):
    smem = pl.BlockSpec(memory_space=pltpu.SMEM)
    vmem = pl.BlockSpec(memory_space=pltpu.VMEM)
    cols = KV_HEADS * HEAD
    return pl.pallas_call(
        finish_kernel,
        out_shape=(
            jax.ShapeDtypeStruct((FEATS, NY * cols), jnp.float32),
            jax.ShapeDtypeStruct((FEATS, cols), jnp.float32),
            jax.ShapeDtypeStruct((FEATS, cols), jnp.float32),
        ),
        in_specs=[smem] + [vmem] * len(pieces),
        out_specs=(vmem, vmem, vmem),
        compiler_params=pltpu.CompilerParams(vmem_limit_bytes=VMEM),
        name="finish",
    )(ids, *pieces)


def shift(value, axis, n, s):
    return lax.ppermute(value, axis, [(i, (i + s) % n) for i in range(n)])


def by_head(value, copies):
    return jnp.broadcast_to(value.reshape(ROWS, KV_HEADS, 1, HEAD), (ROWS, KV_HEADS, copies, HEAD)).reshape(
        ROWS, KV_HEADS * copies, HEAD
    )


def gather_x(value):
    return [value] + [shift(value, "x", NX, s) for s in range(1, NX)]


def other_core(values):
    rest = shift(jnp.concatenate(values[1:], axis=0), "c", NC, 1)
    n = values[0].shape[0]
    return [shift(values[0], "c", NC, 1)] + [rest[i * n : (i + 1) * n] for i in range(len(values) - 1)]


def shards(x, q, k, v, do, lens, span):
    ids = jnp.stack([lax.axis_index(a) for a in ("zh", "c", "x", "y", "zl")]).astype(jnp.int32)
    groups = NY * NC
    kv_rows = jnp.concatenate([k, v], axis=1)
    send = jnp.concatenate(
        [q.reshape(ROWS, groups, 2 * HEAD), do.reshape(ROWS, groups, 2 * HEAD)], axis=2
    ).transpose(1, 0, 2)
    kv_rows, x, send = lax.optimization_barrier((kv_rows, x, send))
    own = lax.all_to_all(send, ("y", "c"), 0, 0, tiled=True)
    far = shift(kv_rows, "zh", NZH, 1)

    keep, give = turn(ids, x)
    pair = jnp.concatenate([keep, shift(give, "c", NC, 1)], axis=2)
    quarters = [pair[0]] + [shift(pair[t], "x", NX, t) for t in range(1, NX)]
    send = jnp.stack([kv_rows, far]).reshape(NC, ROWS, 2, KV_HEADS, HEAD)
    send = send.transpose(3, 0, 1, 2, 4).reshape(groups, ROWS, 2 * HEAD)
    own, send, *quarters = lax.optimization_barrier((own, send, *quarters))
    xa, xb = (
        jnp.concatenate([t[h * FEATS : (h + 1) * FEATS] for t in quarters], axis=1) for h in range(NZH)
    )
    kv = lax.all_to_all(send, ("y", "c"), 0, 0, tiled=True)
    kv_got = shift(kv, "c", NC, 1)

    xa_up, xb_up = shift(xa, "y", NY, 1), shift(xb, "y", NY, 1)
    xa_down, xb_down = shift(xa, "y", NY, -1), shift(xb, "y", NY, -1)
    dq, kept, given = attention(ids, span, lens, own, kv, kv_got)
    dq, kept, given, xa_up, xb_down, xa_down, xb_up = lax.optimization_barrier(
        (dq, kept, given, xa_up, xb_down, xa_down, xb_up)
    )
    dqs = gather_x(dq)
    both = kept.astype(jnp.float32) + shift(given, "c", NC, 1).astype(jnp.float32)
    both, xa_up = lax.optimization_barrier((both, xa_up))
    xa_far = shift(xa_up, "y", NY, 1)
    got = shift(both[OWN:].astype(jnp.bfloat16), "zh", NZH, 1)
    dqs[1], xb_down = lax.optimization_barrier((dqs[1], xb_down))
    xb_far = shift(xb_down, "y", NY, -1)
    got, xb_far, *dqs = lax.optimization_barrier((got, xb_far, *dqs))
    xa_far, *dqs = lax.optimization_barrier((xa_far, *dqs))
    x_all = [xa, xa_up, xa_down, xa_far, xb, xb_up, xb_down, xb_far]
    mine = (both[:OWN] + got.astype(jnp.float32)).astype(jnp.bfloat16)
    mines = gather_x(mine)
    part = weight_term(ids, x_all, dqs, other_core(dqs))
    part, *mines = lax.optimization_barrier((part, *mines))
    part = weight_term(ids, x_all, mines, other_core(mines), part)
    sub, cols = part.shape[-2:]
    got = lax.all_to_all(part.reshape(NZH * NZL * NY, sub, cols), ("zh", "zl", "y"), 0, 0, tiled=True)
    got = got.reshape(NZH * NZL, NY, sub, cols)
    piece = jnp.sum(got.astype(jnp.float32), axis=0).astype(jnp.bfloat16)
    line = jnp.stack([piece] + [shift(piece, "zl", NZL, s) for s in range(1, NZL)])
    pieces = [line] + [shift(line, "x", NX, s) for s in range(1, NX)]
    return finish(ids, pieces)


def solution(mesh):
    fine = Mesh(mesh.devices.reshape(NX, NZL, NZH, NY, NC), AXES)
    rows = P(AXES, None)
    out = P(("zh", "y", "c"), None)
    return jax.shard_map(
        shards,
        mesh=fine,
        in_specs=(rows, rows, rows, rows, rows, P(("x", "zl"), None), P()),
        out_specs=(out, out, out),
        check_vma=False,
    )
```
